512 devices in a mesh: ctx: 64 (over z, x, core), head: 8 (over y).
Axes of the slice: x: 4, y: 8, z: 8, core: 2. Of those that a mesh axis runs over, the one named last changes fastest.
Arguments:
- context_query: bfloat16 [32768, 8192], P('ctx', 'head'), may hold values from -15 to 15
- context_key: bfloat16 [32768, 1024], P('ctx', 'head'), may hold values from -6 to 6
- context_value: bfloat16 [32768, 1024], P('ctx', 'head'), may hold values from -6 to 6
- request_query: bfloat16 [16384, 8192], P('ctx', 'head'), may hold values from -15 to 15, as said below
- request_key: bfloat16 [16384, 1024], P('ctx', 'head'), may hold values from -6 to 6, as said below
- request_value: bfloat16 [16384, 1024], P('ctx', 'head'), may hold values from -6 to 6
- output_weight: bfloat16 [8192, 8192], P('head', 'ctx'), may hold values from -0.375 to 0.375
- block_lengths: int32 [64], replicated, may hold values from 1 to 512, 24576 in all
- query_host: int32 [1], replicated, may hold values from 0 to 63
Outputs:
- encoded_context: bfloat16 [32768, 8192], P('ctx', 'head')
- request_output: bfloat16 [256, 8192], P('head', 'ctx')
The draws below stay inside these ranges and needn't reach their ends.
Inputs may be any that keep to these rules, and one draw needn't show every extreme that they name: `request_query`: only the slot of host query_host[0] is read. `request_key`: only the slot of host query_host[0] is read. `block_lengths`: one entry a host; the largest is exactly 512; together they are 24576.
All inputs are finite; a program needn't handle non-finite values.
Results may differ from the reference program's by a relative error of at most 0.019.
Values may be sent and summed in bfloat16 or wider, within the bound.
No kernel may reach another device: no remote copies, remote signals or barrier semaphores. Data moves between devices by JAX's collectives and lax.ppermute only.
A program may use at most 192 MiB of HBM per device.

```python
import math
import jax
import jax.numpy as jnp
import numpy as np
from jax import lax

D = 8192
HQ = 64
HK = 8
HD = 128
BLOCK = 512
QUERY = 256
CONTEXT = 32768
SLOTS = 16384
N_CTX = 64


def drawn_rows(key, row_count, col_count, spread):
    return jax.random.truncated_normal(key, -6.0, 6.0, (row_count, col_count), jnp.float32) * spread


def draw_context_query(key, part):
    key = jax.random.fold_in(key, 11)
    return drawn_rows(key, CONTEXT, HQ * HD, 2.5).astype(jnp.bfloat16)


def draw_context_key(key, part):
    key = jax.random.fold_in(key, 23)
    return drawn_rows(key, CONTEXT, HK * HD, 1.0).astype(jnp.bfloat16)


def draw_request_query(key, part):
    key = jax.random.fold_in(key, 37)
    return drawn_rows(key, SLOTS, HQ * HD, 2.5).astype(jnp.bfloat16)


def draw_request_key(key, part):
    key = jax.random.fold_in(key, 41)
    return drawn_rows(key, SLOTS, HK * HD, 1.0).astype(jnp.bfloat16)


def steps_of(key, shape, shards, smallest, largest):
    def one(position, shards_of):
        draws = jax.random.uniform(jax.random.fold_in(jax.random.fold_in(key, 6), position), (shards_of,), jnp.float32, smallest / len(shards), largest / len(shards))
        return jnp.repeat(jnp.exp(draws), shape[position] // shards_of).reshape((-1,) + (1,) * (len(shape) - position - 1))

    level = one(*shards[0])
    for cut in shards[1:]:
        level = level * one(*cut)
    return level


def profile(amount, total, bound, slope):
    portions = [(1 << 20) // math.isqrt(rank ** slope) + 1 for rank in range(2, amount + 1)]
    rest, given = total - bound - (amount - 1), [1] * (amount - 1)
    while rest > 0:
        movable = [i for i in range(amount - 1) if given[i] < bound]
        pool, left = sum([portions[i] for i in movable]), rest
        for i in movable:
            more = min(bound - given[i], max(1, left * portions[i] // pool), rest)
            given[i] = given[i] + more
            rest = rest - more
    return np.array([bound] + given)


def ragged(rng, count, total, most, skew):
    if count == 2:
        one = jax.random.randint(rng, (), max(1, total - most), min(most, total - 1) + 1)
        return jnp.stack([one, total - one])
    lengths = jnp.asarray(profile(count, total, most, skew), jnp.int32)
    twos = (count - 1) // 2
    donor, receiver = lengths[1:1 + 2 * twos:2], lengths[2:2 + 2 * twos:2]
    slack = jnp.minimum(donor - 1, most - receiver)
    shifted = jax.random.randint(jax.random.fold_in(rng, 1), (twos,), 0, 1 << 20) % (slack + 1)
    lengths = lengths.at[1:1 + 2 * twos:2].set(donor - shifted).at[2:2 + 2 * twos:2].set(receiver + shifted)
    return lengths[jax.random.permutation(jax.random.fold_in(rng, 2), count)]


def bell_draw(stream_key, shape, width, most, pieces=(), held_as=jnp.bfloat16):
    gain = steps_of(stream_key, shape, pieces, -0.22, 0.18) if pieces else 1.0
    values = jax.random.normal(stream_key, shape, jnp.float32) * width * gain
    return jnp.minimum(jnp.maximum(values, -most), most).astype(held_as)


def setup_inputs(seed: int = 0) -> dict:
    seeds = jax.random.split(jax.random.key(seed), 10)
    return {
        "context_query": draw_context_query(jax.random.fold_in(seeds[9], 71), 0),
        "context_key": draw_context_key(jax.random.fold_in(seeds[9], 71), 0),
        "context_value": bell_draw(seeds[2], (CONTEXT, HK * HD), 1.0, 6.0, ((0, 64), (1, 8))),
        "request_query": draw_request_query(jax.random.fold_in(seeds[9], 71), 0),
        "request_key": draw_request_key(jax.random.fold_in(seeds[9], 71), 0),
        "request_value": bell_draw(seeds[5], (SLOTS, HK * HD), 1.0, 6.0, ((0, 64), (1, 8))),
        "output_weight": bell_draw(seeds[6], (HQ * HD, D), (2 * HD) ** -0.5, 0.375, ((0, 8), (1, 64))),
        "block_lengths": ragged(seeds[7], N_CTX, CONTEXT * 3 // 4, BLOCK, 0).astype(jnp.int32),
        "query_host": jax.random.randint(seeds[8], (1,), 0, N_CTX).astype(jnp.int32),
    }


def partial_terms(queries, key_rows, value_rows, seen_mask):
    query_count = queries.shape[0]
    key_count = key_rows.shape[0]
    query_heads = queries.astype(jnp.float32).reshape(query_count, HK, HQ // HK, HD)
    key_heads = key_rows.astype(jnp.float32).reshape(key_count, HK, HD)
    value_heads = value_rows.astype(jnp.float32).reshape(key_count, HK, HD)
    scores = jnp.einsum("rkgd,skd->rkgs", query_heads, key_heads) * HD ** -0.5
    scores = jnp.where(seen_mask[:, None, None, :], scores, -jnp.inf)
    row_peak = jnp.max(scores, axis=3)
    weights = jnp.exp(scores - row_peak[..., None]).astype(jnp.bfloat16)
    weights = lax.optimization_barrier(weights).astype(jnp.float32)
    row_total = jnp.sum(weights, axis=3)
    row_values = jnp.einsum("rkgs,skd->rkgd", weights, value_heads)
    return row_peak, row_total, row_values


def reference(context_query, context_key, context_value, request_query, request_key, request_value, output_weight, block_lengths, query_host):
    anchor_len = block_lengths[0]
    anchor_key = context_key[:BLOCK]
    anchor_value = context_value[:BLOCK]
    line_ids = jnp.arange(BLOCK, dtype=jnp.int32)
    own_order = line_ids[None, :] <= line_ids[:, None]

    def encode(host_index):
        start_row = (host_index * BLOCK).astype(jnp.int32)
        block_query = lax.dynamic_slice_in_dim(context_query, start_row, BLOCK, 0)
        block_key = lax.dynamic_slice_in_dim(context_key, start_row, BLOCK, 0)
        block_value = lax.dynamic_slice_in_dim(context_value, start_row, BLOCK, 0)
        own_len = block_lengths[host_index]
        own_seen = own_order & (line_ids[None, :] < own_len)
        anchor_seen = jnp.broadcast_to((line_ids[None, :] < anchor_len) & (host_index > 0), (BLOCK, BLOCK))
        seen_mask = jnp.concatenate([anchor_seen, own_seen], axis=1)
        row_peak, row_total, row_values = partial_terms(
            block_query,
            jnp.concatenate([anchor_key, block_key], axis=0),
            jnp.concatenate([anchor_value, block_value], axis=0),
            seen_mask)
        encoded = (row_values / row_total[..., None]).reshape(BLOCK, HQ * HD)
        live_rows = line_ids[:, None] < own_len
        return jnp.where(live_rows, encoded, 0.0).astype(jnp.bfloat16)

    encoded_context = lax.map(encode, jnp.arange(N_CTX, dtype=jnp.int32)).reshape(CONTEXT, HQ * HD)

    slot_host = query_host[0]
    start_slot = (slot_host * QUERY).astype(jnp.int32)
    asked_query = lax.dynamic_slice_in_dim(request_query, start_slot, QUERY, 0)
    asked_key = lax.dynamic_slice_in_dim(request_key, start_slot, QUERY, 0)
    asked_value = lax.dynamic_slice_in_dim(request_value, start_slot, QUERY, 0)
    slot_ids = jnp.arange(QUERY, dtype=jnp.int32)
    self_order = slot_ids[None, :] <= slot_ids[:, None]

    def absorb(carry, host_index):
        global_peak, denom_sum, numer_sum = carry
        start_row = (host_index * BLOCK).astype(jnp.int32)
        block_key = lax.dynamic_slice_in_dim(context_key, start_row, BLOCK, 0)
        block_value = lax.dynamic_slice_in_dim(context_value, start_row, BLOCK, 0)
        own_len = block_lengths[host_index]
        block_seen = jnp.broadcast_to(line_ids[None, :] < own_len, (QUERY, BLOCK))
        self_seen = self_order & (host_index == slot_host)
        row_peak, row_total, row_values = partial_terms(
            asked_query,
            jnp.concatenate([block_key, asked_key], axis=0),
            jnp.concatenate([block_value, asked_value], axis=0),
            jnp.concatenate([block_seen, self_seen], axis=1))
        new_peak = jnp.maximum(global_peak, row_peak)
        keep_old = jnp.exp(global_peak - new_peak)
        keep_new = jnp.exp(row_peak - new_peak)
        denom_sum = denom_sum * keep_old + row_total * keep_new
        numer_sum = numer_sum * keep_old[..., None] + row_values * keep_new[..., None]
        return (new_peak, denom_sum, numer_sum), host_index

    start_state = (
        jnp.full((QUERY, HK, HQ // HK), -jnp.inf, jnp.float32),
        jnp.zeros((QUERY, HK, HQ // HK), jnp.float32),
        jnp.zeros((QUERY, HK, HQ // HK, HD), jnp.float32))
    final_state, visited = lax.scan(absorb, start_state, jnp.arange(N_CTX, dtype=jnp.int32))
    numer_sum = final_state[2]
    denom_sum = final_state[1]
    attended = (numer_sum / denom_sum[..., None]).reshape(QUERY, HQ * HD).astype(jnp.bfloat16)
    request_output = jnp.dot(attended, output_weight, preferred_element_type=jnp.float32).astype(jnp.bfloat16)
    return encoded_context, request_output
```

```python
import jax
import jax.numpy as jnp
from jax import lax
from jax.experimental import pallas as pl
from jax.experimental.pallas import tpu as pltpu
from jax.sharding import Mesh, PartitionSpec as P

HD = 128
HEADS = 8
HALF = HEADS // 2
BLOCK = 512
QUERY = 256
Z, X, C = 8, 4, 2
SCALE = HD ** (-0.5) * 1.4426950408889634
NEG = -1e30
BF16 = jnp.bfloat16
F32 = jnp.float32
CHIPS = ("z", "x")


def params(**extra):
    return pltpu.CompilerParams(vmem_limit_bytes=32 * 1024 * 1024, **extra)


def smem():
    return pl.BlockSpec(memory_space=pltpu.SMEM)


def vmem():
    return pl.BlockSpec(memory_space=pltpu.VMEM)


def weigh(query, parts):
    scores = []
    for keys, _, seen in parts:
        score = lax.dot_general(query, keys, (((1,), (1,)), ((), ())), preferred_element_type=F32)
        scores.append(score if seen is None else jnp.where(seen, score, NEG))
    peak = scores[0].max(axis=1, keepdims=True)
    for score in scores[1:]:
        peak = jnp.maximum(peak, score.max(axis=1, keepdims=True))
    total = None
    for score, (_, values, _) in zip(scores, parts):
        weights = jnp.exp2((score - peak) * SCALE).astype(BF16)
        term = jnp.dot(weights, values, preferred_element_type=F32)
        total = term if total is None else total + term
    return peak, total[:, :HD], total[:, HD:]


def with_ones(values):
    return jnp.concatenate([values, jnp.ones(values.shape, BF16)], axis=1)


def column_ids(rows, cols):
    return lax.broadcasted_iota(jnp.int32, (rows, cols), 1)


def causal(size):
    return column_ids(size, size) <= lax.broadcasted_iota(jnp.int32, (size, size), 0)


def pack_kernel(query, key, value, ask_key, ask_value, to_core, to_pair):
    pieces, piece_rows = to_core.shape[1], HALF * QUERY // to_core.shape[1]
    per_head = pieces // HALF
    extra = BLOCK // pieces
    for core, rows in ((0, key), (1, value)):
        for head in range(HALF):
            column = (core * HALF + head) * HD
            to_core[core, head * per_head : (head + 1) * per_head, :piece_rows, :] = query[
                :, column : column + HD
            ].reshape(per_head, piece_rows, HD)
        to_core[core, :, piece_rows:, :] = rows[...].reshape(pieces, extra, HD)
    to_pair[0:BLOCK, :] = key[...]
    to_pair[BLOCK : 2 * BLOCK, :] = value[...]
    to_pair[2 * BLOCK : 2 * BLOCK + QUERY, :] = ask_key[...]
    to_pair[2 * BLOCK + QUERY :, :] = ask_value[...]


def pack(query, key, value, ask_key, ask_value, pieces):
    rows = (HALF * QUERY + BLOCK) // pieces
    return pl.pallas_call(
        pack_kernel,
        out_shape=(
            jax.ShapeDtypeStruct((C, pieces, rows, HD), BF16),
            jax.ShapeDtypeStruct((2 * BLOCK + 2 * QUERY, HD), BF16),
        ),
        in_specs=[vmem()] * 5,
        out_specs=(vmem(), vmem()),
        compiler_params=params(),
        name="pack",
    )(query, key, value, ask_key, ask_value)


def choose_kernel(which, asked, anchor, out):
    split = HALF * QUERY // (out.shape[-3])
    out[:, :split, :] = asked[0, :, :split, :]
    out[:, split:, :] = anchor[0, :, split:, :]


def choose(which, received):
    shape = received.shape[1:]
    return pl.pallas_call(
        choose_kernel,
        out_shape=jax.ShapeDtypeStruct(shape, BF16),
        grid_spec=pltpu.PrefetchScalarGridSpec(
            num_scalar_prefetch=1,
            grid=(1,),
            in_specs=[
                pl.BlockSpec((1,) + shape, lambda i, which: (which[0], 0, 0, 0)),
                pl.BlockSpec((1,) + shape, lambda i, which: (0, 0, 0, 0)),
            ],
            out_specs=pl.BlockSpec(shape, lambda i, which: (0, 0, 0)),
        ),
        compiler_params=params(),
        name="choose",
    )(which, received, received)


def spread_kernel(which, asked, anchor, out):
    split = HALF * QUERY // out.shape[0]
    out[:, :split, :] = jnp.broadcast_to(asked[:, :split, :], (out.shape[0], split, HD))
    out[:, split:, :] = jnp.broadcast_to(anchor[:, split:, :], (out.shape[0], out.shape[1] - split, HD))


def spread(which, received):
    pieces, rows, _ = received.shape
    return pl.pallas_call(
        spread_kernel,
        out_shape=jax.ShapeDtypeStruct(received.shape, BF16),
        grid_spec=pltpu.PrefetchScalarGridSpec(
            num_scalar_prefetch=1,
            grid=(1,),
            in_specs=[
                pl.BlockSpec((1, rows, HD), lambda i, which: (which[0], 0, 0)),
                pl.BlockSpec((1, rows, HD), lambda i, which: (0, 0, 0)),
            ],
            out_specs=pl.BlockSpec(received.shape, lambda i, which: (0, 0, 0)),
        ),
        compiler_params=params(),
        name="spread",
    )(which, received, received)


def ask_kernel(meta, query, rows, out, values):
    pieces, piece_rows = query.shape[0], HALF * QUERY // query.shape[0]
    per_head = pieces // HALF
    for core in range(C):
        values[core * BLOCK : (core + 1) * BLOCK, :] = with_ones(rows[core, BLOCK : 2 * BLOCK, :])

    def run(own):
        for head in range(HALF):
            asked = query[head * per_head : (head + 1) * per_head, :piece_rows, :].reshape(QUERY, HD)
            parts = [
                (
                    rows[core, 0:BLOCK, :],
                    values[core * BLOCK : (core + 1) * BLOCK, :],
                    column_ids(QUERY, BLOCK) < meta[core],
                )
                for core in range(C)
            ]
            if own:
                ask_key = rows[meta[3], 2 * BLOCK : 2 * BLOCK + QUERY, :]
                ask_value = with_ones(rows[meta[3], 2 * BLOCK + QUERY :, :])
                parts.append((ask_key, ask_value, causal(QUERY)))
            peak, numer, denom = weigh(asked, parts)
            out[head * per_head : (head + 1) * per_head, :piece_rows, :] = (
                (numer / denom).astype(BF16).reshape(per_head, piece_rows, HD)
            )
            level = peak * SCALE + jnp.log2(denom)
            high = level.astype(BF16)
            rest = level - high.astype(F32)
            middle = rest.astype(BF16)
            low = (rest - middle.astype(F32)).astype(BF16)
            lane = column_ids(QUERY, HD) % (HD // 2)
            coded = jnp.where(lane == 0, high.astype(F32), jnp.where(lane == 1, middle.astype(F32), low.astype(F32)))
            coded = coded.reshape(per_head, piece_rows, HD)
            left = column_ids(piece_rows // 2, HD) < HD // 2
            coded = jnp.where(left[None], coded[:, : piece_rows // 2, :], coded[:, piece_rows // 2 :, :])
            out[head * per_head : (head + 1) * per_head, piece_rows:, :] = coded.astype(BF16)

    @pl.when(meta[2] == 0)
    def _():
        run(False)

    @pl.when(meta[2] != 0)
    def _():
        run(True)


def ask(meta, query, rows):
    pieces = query.shape[0]
    piece_rows = HALF * QUERY // pieces
    return pl.pallas_call(
        ask_kernel,
        out_shape=jax.ShapeDtypeStruct((pieces, piece_rows + piece_rows // 2, HD), BF16),
        in_specs=[smem(), vmem(), vmem()],
        out_specs=vmem(),
        scratch_shapes=[pltpu.VMEM((C * BLOCK, 2 * HD), BF16)],
        compiler_params=params(),
        name="ask",
    )(meta, query, rows)


def merge_kernel(received, out):
    pieces, piece_rows = out.shape[0], out.shape[1]
    half = piece_rows // 2
    levels = []
    for piece in range(pieces):
        coded = received[piece, piece_rows:, :].astype(F32)
        first = coded[:, 0:1] + coded[:, 1:2] + coded[:, 2:3]
        second = coded[:, 64:65] + coded[:, 65:66] + coded[:, 66:67]
        levels.append(jnp.concatenate([first, second], axis=0))
    top = levels[0]
    for level in levels[1:]:
        top = jnp.maximum(top, level)
    numer = jnp.zeros((piece_rows, HD), F32)
    denom = jnp.zeros((piece_rows, 1), F32)
    for piece, level in enumerate(levels):
        share = jnp.exp2(level - top)
        numer += share * received[piece, :piece_rows, :].astype(F32)
        denom += share
    merged = (numer / denom).astype(BF16)
    out[...] = jnp.broadcast_to(merged[None], out.shape)


def merge(received):
    pieces = received.shape[0]
    return pl.pallas_call(
        merge_kernel,
        out_shape=jax.ShapeDtypeStruct((pieces, HALF * QUERY // pieces, HD), BF16),
        in_specs=[vmem()],
        out_specs=vmem(),
        compiler_params=params(),
        name="merge",
    )(received)


def project_kernel(attended, weight, out):
    total = jnp.zeros((QUERY, HD), F32)
    for head in range(HEADS):
        total += jnp.dot(
            attended[head * QUERY : (head + 1) * QUERY, :],
            weight[head * HD : (head + 1) * HD, :],
            preferred_element_type=F32,
        )
    out[...] = total.astype(BF16)


def project(attended, weight):
    return pl.pallas_call(
        project_kernel,
        out_shape=jax.ShapeDtypeStruct((QUERY, HD), BF16),
        in_specs=[vmem(), vmem()],
        out_specs=vmem(),
        compiler_params=params(),
        name="project",
    )(attended, weight)


def encode_kernel(meta, query, key, value, anchor, out, own_values, anchor_values):
    @pl.when(pl.program_id(0) == 0)
    def _():
        own_values[...] = with_ones(value[...])
        anchor_values[...] = with_ones(anchor[BLOCK:, :])

    own_len, anchor_len = meta[4], meta[5]
    half = BLOCK // 2
    for tile in range(2):
        rows = slice(tile * half, (tile + 1) * half)
        parts = [
            (key[rows, :], own_values[rows, :], causal(half)),
            (anchor[:BLOCK, :], anchor_values[...], column_ids(half, BLOCK) < anchor_len),
        ]
        if tile:
            parts.append((key[:half, :], own_values[:half, :], None))
        _, numer, denom = weigh(query[rows, :], parts)
        live = lax.broadcasted_iota(jnp.int32, (half, HD), 0) + tile * half < own_len
        out[rows, :] = jnp.where(live, numer / denom, 0.0).astype(BF16)


def encode(meta, query, key, value, anchor):
    return pl.pallas_call(
        encode_kernel,
        out_shape=jax.ShapeDtypeStruct(query.shape, BF16),
        grid=(HEADS,),
        in_specs=[
            smem(),
            pl.BlockSpec((BLOCK, HD), lambda h: (0, h)),
            pl.BlockSpec((BLOCK, HD), lambda h: (0, 0)),
            pl.BlockSpec((BLOCK, HD), lambda h: (0, 0)),
            pl.BlockSpec((2 * BLOCK, HD), lambda h: (0, 0)),
        ],
        out_specs=pl.BlockSpec((BLOCK, HD), lambda h: (0, h)),
        scratch_shapes=[pltpu.VMEM((BLOCK, 2 * HD), BF16)] * 2,
        compiler_params=params(),
        cost_estimate=pl.CostEstimate(
            flops=HEADS * BLOCK * BLOCK * HD * 8,
            bytes_accessed=5 * BLOCK * HEADS * HD,
            transcendentals=HEADS * BLOCK * BLOCK * 2,
        ),
        name="encode",
    )(meta, query, key, value, anchor)


def body(
    context_query,
    context_key,
    context_value,
    request_query,
    request_key,
    request_value,
    output_weight,
    block_lengths,
    query_host,
):
    pieces = Z * X
    chip = lax.axis_index("z") * X + lax.axis_index("x")
    host = chip * C + lax.axis_index("c")
    source = query_host[0]
    source_chip, source_core = source // C, source % C
    pair_lens = lax.dynamic_slice_in_dim(block_lengths, chip * C, C, 0)
    own_len = lax.dynamic_index_in_dim(block_lengths, host, 0, keepdims=False)
    meta = jnp.stack(
        [
            pair_lens[0],
            pair_lens[1],
            (chip == source_chip).astype(jnp.int32),
            source_core,
            own_len,
            jnp.where(host > 0, block_lengths[0], 0),
        ]
    )

    to_core, to_pair = pack(request_query, context_key, context_value, request_key, request_value, pieces)
    pair_rows = lax.all_gather(to_pair, "c", axis=0)
    from_core = lax.all_to_all(to_core, "c", 0, 0)
    to_chips = choose(source_core[None], from_core)
    from_chips = lax.all_to_all(to_chips, CHIPS, 0, 0, tiled=True)
    part = spread(source_chip[None], from_chips)
    queries = lax.all_to_all(part, CHIPS, 0, 0, tiled=True)
    anchor = lax.all_gather(queries[:, HALF * QUERY // pieces :, :].reshape(BLOCK, HD), "c", axis=0, tiled=True)

    sums = ask(meta, queries, pair_rows)
    met = lax.all_to_all(sums, CHIPS, 0, 0, tiled=True)
    merged = lax.all_to_all(merge(met), CHIPS, 0, 0, tiled=True)
    attended = lax.all_gather(merged.reshape(HALF * QUERY, HD), "c", axis=0, tiled=True)
    shares = project(attended, output_weight).reshape(-1, QUERY // lax.axis_size("head"), HD)
    shares = lax.all_to_all(shares, "head", 0, 0, tiled=True)
    request_output = jnp.sum(shares.astype(F32), axis=0).astype(BF16)

    encoded_context = encode(meta, context_query, context_key, context_value, anchor)
    return (encoded_context, request_output)


def solution(mesh):
    fine = Mesh(mesh.devices.reshape(Z, X, C, -1), ("z", "x", "c", "head"))
    ctx = ("z", "x", "c")
    placed = (P(ctx, "head"),) * 6 + (P("head", ctx), P(), P())
    return jax.shard_map(
        body,
        mesh=fine,
        in_specs=placed,
        out_specs=(P(ctx, "head"), P("head", ctx)),
        check_vma=False,
    )
```

```python
import jax
import jax.numpy as jnp
from jax import lax
from jax.experimental import pallas as pl
from jax.experimental.pallas import tpu as pltpu
from jax.sharding import Mesh, PartitionSpec as P

HD = 128
HEADS = 8
HALF = HEADS // 2
BLOCK = 512
QUERY = 256
Z, X, C = 8, 4, 2
SCALE = HD ** (-0.5) * 1.4426950408889634
NEG = -1e30
GROUPS = 4
BF16 = jnp.bfloat16
F32 = jnp.float32
CHIPS = ("z", "x")


def params(mib=32):
    return pltpu.CompilerParams(vmem_limit_bytes=mib * 1024 * 1024)


def smem():
    return pl.BlockSpec(memory_space=pltpu.SMEM)


def vmem():
    return pl.BlockSpec(memory_space=pltpu.VMEM)


def weigh(query, parts):
    scores = []
    for keys, _, seen in parts:
        score = lax.dot_general(query, keys, (((1,), (1,)), ((), ())), preferred_element_type=F32)
        scores.append(score if seen is None else jnp.where(seen, score, NEG))
    peak = scores[0].max(axis=1, keepdims=True)
    for score in scores[1:]:
        peak = jnp.maximum(peak, score.max(axis=1, keepdims=True))
    total = None
    for score, (_, values, _) in zip(scores, parts):
        weights = jnp.exp2((score - peak) * SCALE).astype(BF16)
        term = jnp.dot(weights, values, preferred_element_type=F32)
        total = term if total is None else total + term
    return peak, total[:, :HD], total[:, HD:]


def with_ones(values):
    return jnp.concatenate([values, jnp.ones(values.shape, BF16)], axis=1)


def column_ids(rows, cols):
    return lax.broadcasted_iota(jnp.int32, (rows, cols), 1)


def causal(size):
    return column_ids(size, size) <= lax.broadcasted_iota(jnp.int32, (size, size), 0)


def piece_rows():
    return QUERY // Z


def anchor_rows():
    return BLOCK // (Z * X)


def level_rows():
    return piece_rows() // GROUPS


def pack_kernel(host, query, key, value, send, keep):
    core = host[0] % C
    for out, half in ((send, 1 - core), (keep, core)):
        for head in range(HALF):
            column = pl.multiple_of((half * HALF + head) * HD, HD)
            out[:, head, : piece_rows(), :] = query[:, pl.ds(column, HD)].reshape(Z, piece_rows(), HD)

        @pl.when(half == 0)
        def _():
            out[:, :, piece_rows() :, :] = key[...].reshape(Z, X, anchor_rows(), HD)

        @pl.when(half == 1)
        def _():
            out[:, :, piece_rows() :, :] = value[...].reshape(Z, X, anchor_rows(), HD)


def pack(host, query, key, value):
    shape = (Z, X, piece_rows() + anchor_rows(), HD)
    return pl.pallas_call(
        pack_kernel,
        out_shape=(jax.ShapeDtypeStruct(shape, BF16),) * 2,
        grid=(1,),
        in_specs=[smem()] + [pl.BlockSpec(a.shape, lambda i: (0, 0)) for a in (query, key, value)],
        out_specs=(pl.BlockSpec(shape, lambda i: (0, 0, 0, 0)),) * 2,
        compiler_params=params(60),
        name="pack",
    )(host, query, key, value)


def join_kernel(*refs):
    out, row = refs[-1], 0
    for ref in refs[:-1]:
        out[row : row + ref.shape[0], :] = ref[...]
        row += ref.shape[0]


def join(*arrays):
    rows = sum(a.shape[0] for a in arrays)
    return pl.pallas_call(
        join_kernel,
        out_shape=jax.ShapeDtypeStruct((rows, HD), BF16),
        grid=(1,),
        in_specs=[pl.BlockSpec(a.shape, lambda i: (0, 0)) for a in arrays],
        out_specs=pl.BlockSpec((rows, HD), lambda i: (0, 0)),
        compiler_params=params(),
        name="join",
    )(*arrays)


def choose_kernel(host, source, kept, received, out):
    core = host[0] % C
    split = piece_rows()
    for part, mine in ((slice(0, split), source[0] % C == core), (slice(split, out.shape[2]), core == 0)):

        @pl.when(mine)
        def _():
            out[:, :, part, :] = kept[:, :, part, :]

        @pl.when(jnp.logical_not(mine))
        def _():
            out[:, :, part, :] = received[:, :, part, :]


def choose(host, source, kept, received):
    spec = pl.BlockSpec(kept.shape, lambda i: (0, 0, 0, 0))
    return pl.pallas_call(
        choose_kernel,
        out_shape=jax.ShapeDtypeStruct(kept.shape, BF16),
        grid=(1,),
        in_specs=[smem(), smem(), spec, spec],
        out_specs=spec,
        compiler_params=params(),
        name="choose",
    )(host, source, kept, received)


def spread_kernel(source, asked, anchor, out):
    split = piece_rows()
    out[:, :split, :] = jnp.broadcast_to(asked[:, :split, :], (out.shape[0], split, HD))
    out[:, split:, :] = jnp.broadcast_to(anchor[:, split:, :], (out.shape[0], out.shape[1] - split, HD))


def spread(source, received):
    pieces, rows, _ = received.shape
    return pl.pallas_call(
        spread_kernel,
        out_shape=jax.ShapeDtypeStruct(received.shape, BF16),
        grid_spec=pltpu.PrefetchScalarGridSpec(
            num_scalar_prefetch=1,
            grid=(1,),
            in_specs=[
                pl.BlockSpec((1, rows, HD), lambda i, source: (source[0] // C, 0, 0)),
                pl.BlockSpec((1, rows, HD), lambda i, source: (0, 0, 0)),
            ],
            out_specs=pl.BlockSpec(received.shape, lambda i, source: (0, 0, 0)),
        ),
        compiler_params=params(),
        name="spread",
    )(source, received, received)


def ask_kernel(host, source, lengths, query, rows, out, values):
    split = piece_rows()
    chip = host[0] // C
    for core in range(C):
        values[core] = with_ones(rows[core, BLOCK : 2 * BLOCK, :])

    def run(own):
        for head in range(HALF):
            asked = query[:, head, :split, :].reshape(QUERY, HD)
            parts = [
                (rows[core, :BLOCK, :], values[core], column_ids(QUERY, BLOCK) < lengths[chip * C + core])
                for core in range(C)
            ]
            if own:
                core = source[0] % C
                ask_key = rows[core, 2 * BLOCK : 2 * BLOCK + QUERY, :]
                ask_value = rows[core, 2 * BLOCK + QUERY :, :]
                parts.append((ask_key, with_ones(ask_value), causal(QUERY)))
            peak, numer, denom = weigh(asked, parts)
            out[:, head, :split, :] = (numer / denom).astype(BF16).reshape(Z, split, HD)
            level = peak * SCALE + jnp.log2(denom)
            high = level.astype(BF16).astype(F32)
            rest = level - high
            middle = rest.astype(BF16).astype(F32)
            lane = column_ids(QUERY, HD) % (HD // GROUPS)
            coded = jnp.where(lane == 0, high, jnp.where(lane == 1, middle, rest - middle))
            coded = coded.reshape(Z, GROUPS, level_rows(), HD)
            group = column_ids(level_rows(), HD) // (HD // GROUPS)
            side = coded[:, 0]
            for index in range(1, GROUPS):
                side = jnp.where((group == index)[None], coded[:, index], side)
            out[:, head, split:, :] = side.astype(BF16)

    here = source[0] // C == chip

    @pl.when(jnp.logical_not(here))
    def _():
        run(False)

    @pl.when(here)
    def _():
        run(True)


def ask(host, source, lengths, query, rows):
    return pl.pallas_call(
        ask_kernel,
        out_shape=jax.ShapeDtypeStruct((Z, X, piece_rows() + level_rows(), HD), BF16),
        in_specs=[smem()] * 3 + [vmem()] * 2,
        out_specs=vmem(),
        scratch_shapes=[pltpu.VMEM((C, BLOCK, 2 * HD), BF16)],
        compiler_params=params(),
        cost_estimate=pl.CostEstimate(
            flops=HALF * QUERY * C * BLOCK * HD * 6, bytes_accessed=1 << 20, transcendentals=HALF * QUERY * C * BLOCK
        ),
        name="ask",
    )(host, source, lengths, query, rows)


def merge_kernel(received, out):
    split, step = piece_rows(), level_rows()
    pieces = received.shape[0]
    lane = lax.broadcasted_iota(jnp.int32, (HD, GROUPS * HD), 0)
    column = lax.broadcasted_iota(jnp.int32, (HD, GROUPS * HD), 1)
    width = HD // GROUPS
    adder = ((lane // width == column // HD) & (lane % width < 3)).astype(F32).astype(BF16)
    coded = received[:, split:, :].reshape(pieces * step, HD)
    levels = jnp.dot(coded, adder, preferred_element_type=F32).reshape(pieces, step, GROUPS * HD)
    for group in range(GROUPS):
        level = levels[:, :, group * HD : (group + 1) * HD]
        share = jnp.exp2(level - level.max(axis=0, keepdims=True))
        rows = slice(group * step, (group + 1) * step)
        numer = jnp.sum(share * received[:, rows, :].astype(F32), axis=0)
        merged = (numer / jnp.sum(share, axis=0)).astype(BF16)
        out[:, rows, :] = jnp.broadcast_to(merged[None], (pieces, step, HD))


def merge(received):
    return pl.pallas_call(
        merge_kernel,
        out_shape=jax.ShapeDtypeStruct((received.shape[0], piece_rows(), HD), BF16),
        in_specs=[vmem()],
        out_specs=vmem(),
        compiler_params=params(),
        name="merge",
    )(received)


def project_kernel(host, attended, weight, other, out):
    core = host[0] % C
    rows = [
        jnp.concatenate([attended[z, x] for x in range(X)], axis=1) for z in range(Z)
    ]
    rows = jnp.concatenate(rows, axis=0)
    first = pl.multiple_of(core * HALF * HD, HALF * HD)
    mine = jnp.dot(rows, weight[pl.ds(first, HALF * HD), :], preferred_element_type=F32)
    others = jnp.dot(rows, other[...], preferred_element_type=F32)
    out[pl.ds(core, 1)] = mine.astype(BF16)[None]
    out[pl.ds(1 - core, 1)] = others.astype(BF16)[None]


def project(host, attended, weight, other):
    return pl.pallas_call(
        project_kernel,
        out_shape=jax.ShapeDtypeStruct((C, QUERY, HD), BF16),
        in_specs=[smem()] + [vmem()] * 3,
        out_specs=vmem(),
        compiler_params=params(),
        name="project",
    )(host, attended, weight, other)


def total_kernel(shares, out):
    out[...] = jnp.sum(shares[...].astype(F32), axis=0).astype(BF16)


def total(shares):
    return pl.pallas_call(
        total_kernel,
        out_shape=jax.ShapeDtypeStruct(shares.shape[1:], BF16),
        in_specs=[vmem()],
        out_specs=vmem(),
        compiler_params=params(),
        name="total",
    )(shares)


def encode_kernel(host, lengths, query, key, value, anchor, *rest):
    out, own_values, anchor_values = rest[-3:]

    @pl.when(pl.program_id(0) == 0)
    def _():
        own_values[...] = with_ones(value[...])
        anchor_values[...] = with_ones(anchor[BLOCK:, :])

    own_len = lengths[host[0]]
    anchor_len = jnp.where(host[0] > 0, lengths[0], 0)
    half = BLOCK // 2
    for tile in range(2):
        rows = slice(tile * half, (tile + 1) * half)
        parts = [
            (key[rows, :], own_values[rows, :], causal(half)),
            (anchor[:BLOCK, :], anchor_values[...], column_ids(half, BLOCK) < anchor_len),
        ]
        if tile:
            parts.append((key[:half, :], own_values[:half, :], None))
        _, numer, denom = weigh(query[rows, :], parts)
        live = lax.broadcasted_iota(jnp.int32, (half, HD), 0) + tile * half < own_len
        out[rows, :] = jnp.where(live, numer / denom, 0.0).astype(BF16)


def encode(host, lengths, query, key, value, anchor, first, count, done=None):
    whole = pl.BlockSpec((BLOCK, HD), lambda h: (0, 0))
    heads = pl.BlockSpec((BLOCK, HD), lambda h: (0, h + first))
    given = () if done is None else (done,)
    return pl.pallas_call(
        encode_kernel,
        out_shape=jax.ShapeDtypeStruct(query.shape, BF16),
        grid=(count,),
        in_specs=[smem(), smem(), heads, whole, whole, pl.BlockSpec((2 * BLOCK, HD), lambda h: (0, 0))]
        + [pl.BlockSpec(memory_space=pl.ANY)] * len(given),
        out_specs=heads,
        scratch_shapes=[pltpu.VMEM((BLOCK, 2 * HD), BF16)] * 2,
        input_output_aliases={6: 0} if given else {},
        compiler_params=params(),
        cost_estimate=pl.CostEstimate(
            flops=count * BLOCK * BLOCK * HD * 10,
            bytes_accessed=5 * BLOCK * count * HD,
            transcendentals=count * BLOCK * BLOCK * 2,
        ),
        name="encode",
    )(host, lengths, query, key, value, anchor, *given)


def body(
    context_query,
    context_key,
    context_value,
    request_query,
    request_key,
    request_value,
    output_weight,
    block_lengths,
    query_host,
):
    pieces = Z * X
    core = lax.axis_index("c")
    host = lax.axis_index(("z", "x", "c")).astype(jnp.int32)[None]

    send, keep = pack(host, request_query, context_key, context_value)
    came = lax.ppermute(send, "c", [(0, 1), (1, 0)])
    to_chips = choose(host, query_host, keep, came).reshape(pieces, -1, HD)
    from_chips = lax.all_to_all(to_chips, CHIPS, 0, 0, tiled=True)
    pair_rows = lax.all_gather(join(context_key, context_value, request_key, request_value), "c", axis=0)
    weight_half = lax.dynamic_slice_in_dim(output_weight, (1 - core) * HALF * HD, HALF * HD, 0)
    other_weight = lax.ppermute(weight_half, "c", [(0, 1), (1, 0)])
    from_chips, pair_rows, other_weight = lax.optimization_barrier((from_chips, pair_rows, other_weight))
    part = spread(query_host, from_chips)
    queries = lax.all_to_all(part, CHIPS, 0, 0, tiled=True)

    sums = ask(host, query_host, block_lengths, queries.reshape(Z, X, -1, HD), pair_rows)
    met = lax.all_to_all(sums.reshape(pieces, -1, HD), CHIPS, 0, 0, tiled=True)
    anchor = lax.all_gather(queries[:, piece_rows() :, :].reshape(BLOCK, HD), "c", axis=0, tiled=True)
    context = (host, block_lengths, context_query, context_key, context_value, anchor)
    encoded = encode(*context, 0, HEADS // 2)
    met, encoded = lax.optimization_barrier((met, encoded))
    gathered = lax.all_to_all(merge(met), CHIPS, 0, 0, tiled=True)
    encoded_context = encode(*context, HEADS // 2, HEADS // 2, encoded)
    gathered, encoded_context = lax.optimization_barrier((gathered, encoded_context))
    shares = project(host, gathered.reshape(Z, X, -1, HD), output_weight, other_weight)
    blocks = lax.axis_size("head")
    shares = lax.all_to_all(shares.reshape(C * blocks, -1, HD), ("c", "head"), 0, 0, tiled=True)
    return (encoded_context, total(shares))


def solution(mesh):
    fine = Mesh(mesh.devices.reshape(Z, X, C, -1), ("z", "x", "c", "head"))
    ctx = ("z", "x", "c")
    placed = (P(ctx, "head"),) * 6 + (P("head", ctx), P(), P())
    return jax.shard_map(
        body,
        mesh=fine,
        in_specs=placed,
        out_specs=(P(ctx, "head"), P("head", ctx)),
        check_vma=False,
    )
```

```python
import jax
import jax.numpy as jnp
from jax import lax
from jax.experimental import pallas as pl
from jax.experimental.pallas import tpu as pltpu
from jax.sharding import Mesh, PartitionSpec as P

HD = 128
HEADS = 8
HALF = HEADS // 2
BLOCK = 512
QUERY = 256
Z, X, C = 8, 4, 2
SCALE = HD ** (-0.5) * 1.4426950408889634
NEG = -1e30
GROUPS = 4
BF16 = jnp.bfloat16
F32 = jnp.float32
CHIPS = ("z", "x")


def params(mib=32):
    return pltpu.CompilerParams(vmem_limit_bytes=mib * 1024 * 1024)


def smem():
    return pl.BlockSpec(memory_space=pltpu.SMEM)


def vmem():
    return pl.BlockSpec(memory_space=pltpu.VMEM)


def weigh(query, parts):
    scores = []
    for keys, _, seen in parts:
        score = lax.dot_general(query, keys, (((1,), (1,)), ((), ())), preferred_element_type=F32)
        scores.append(score if seen is None else jnp.where(seen, score, NEG))
    peak = scores[0].max(axis=1, keepdims=True)
    for score in scores[1:]:
        peak = jnp.maximum(peak, score.max(axis=1, keepdims=True))
    total = None
    for score, (_, values, _) in zip(scores, parts):
        weights = jnp.exp2((score - peak) * SCALE).astype(BF16)
        term = jnp.dot(weights, values, preferred_element_type=F32)
        total = term if total is None else total + term
    return peak, total[:, :HD], total[:, HD:]


def with_ones(values):
    return jnp.concatenate([values, jnp.ones(values.shape, BF16)], axis=1)


def column_ids(rows, cols):
    return lax.broadcasted_iota(jnp.int32, (rows, cols), 1)


def causal(size):
    return column_ids(size, size) <= lax.broadcasted_iota(jnp.int32, (size, size), 0)


def piece_rows():
    return QUERY // Z


def anchor_rows():
    return BLOCK // (Z * X)


def level_rows():
    return piece_rows() // GROUPS


def pack_kernel(host, source, query, came, *rest):
    anchors, out = rest[:-1], rest[-1]
    core = host[0] % C
    first = pl.multiple_of(core * HALF * HD, HALF * HD)

    def put(rows):
        for head in range(HALF):
            out[:, head, : piece_rows(), :] = rows[:, pl.ds(first + head * HD, HD)].reshape(Z, piece_rows(), HD)

    here = source[0] % C == core

    @pl.when(here)
    def _():
        put(query)

    @pl.when(jnp.logical_not(here))
    def _():
        put(came)

    for index, rows in enumerate(anchors):

        @pl.when(core == index)
        def _():
            out[:, :, piece_rows() :, :] = rows[...].reshape(Z, X, anchor_rows(), HD)


def pack(host, source, *arrays):
    shape = (Z, X, piece_rows() + anchor_rows(), HD)
    return pl.pallas_call(
        pack_kernel,
        out_shape=jax.ShapeDtypeStruct(shape, BF16),
        in_specs=[smem()] * 2 + [vmem()] * len(arrays),
        out_specs=vmem(),
        compiler_params=params(),
        name="pack",
    )(host, source, *arrays)


def blank_kernel(out):
    pass


def blank():
    shape = (Z, X, piece_rows() + anchor_rows(), HD)
    return pl.pallas_call(
        blank_kernel, out_shape=jax.ShapeDtypeStruct(shape, BF16), out_specs=anywhere(), name="blank"
    )()


def anywhere():
    return pl.BlockSpec(memory_space=pl.ANY)


def join_kernel(*refs):
    out, row = refs[-1], 0
    for ref in refs[:-1]:
        out[row : row + ref.shape[0], :] = ref[...]
        row += ref.shape[0]


def join(*arrays):
    rows = sum(a.shape[0] for a in arrays)
    return pl.pallas_call(
        join_kernel,
        out_shape=jax.ShapeDtypeStruct((rows, HD), BF16),
        grid=(1,),
        in_specs=[pl.BlockSpec(a.shape, lambda i: (0, 0)) for a in arrays],
        out_specs=pl.BlockSpec((rows, HD), lambda i: (0, 0)),
        compiler_params=params(),
        name="join",
    )(*arrays)


def spread_kernel(source, asked, anchor, out):
    split = piece_rows()
    out[:, :split, :] = jnp.broadcast_to(asked[:, :split, :], (out.shape[0], split, HD))
    out[:, split:, :] = jnp.broadcast_to(anchor[:, split:, :], (out.shape[0], out.shape[1] - split, HD))


def spread(source, received):
    pieces, rows, _ = received.shape
    return pl.pallas_call(
        spread_kernel,
        out_shape=jax.ShapeDtypeStruct(received.shape, BF16),
        grid_spec=pltpu.PrefetchScalarGridSpec(
            num_scalar_prefetch=1,
            grid=(1,),
            in_specs=[
                pl.BlockSpec((1, rows, HD), lambda i, source: (source[0] // C, 0, 0)),
                pl.BlockSpec((1, rows, HD), lambda i, source: (0, 0, 0)),
            ],
            out_specs=pl.BlockSpec(received.shape, lambda i, source: (0, 0, 0)),
        ),
        compiler_params=params(),
        name="spread",
    )(source, received, received)


def sideways(rows):
    rows = rows.reshape(Z, GROUPS, level_rows(), HD)
    group = column_ids(level_rows(), HD)[None] // (HD // GROUPS)
    side = rows[:, 0]
    for index in range(1, GROUPS):
        side = jnp.where(group == index, rows[:, index], side)
    return side


def ask_kernel(host, source, meta, query, rows, out, values):
    split = piece_rows()
    chip = host[0] // C
    for core in range(C):
        values[core] = with_ones(rows[core, BLOCK : 2 * BLOCK, :])

    def run(own):
        for head in range(HALF):
            asked = query[:, head, :split, :].reshape(QUERY, HD)
            parts = [
                (rows[core, :BLOCK, :], values[core], column_ids(QUERY, BLOCK) < meta[core])
                for core in range(C)
            ]
            if own:
                core = source[0] % C
                ask_key = rows[core, 2 * BLOCK : 2 * BLOCK + QUERY, :]
                ask_value = rows[core, 2 * BLOCK + QUERY :, :]
                parts.append((ask_key, with_ones(ask_value), causal(QUERY)))
            peak, numer, denom = weigh(asked, parts)
            out[:, head, :split, :] = (numer / denom).astype(BF16).reshape(Z, split, HD)
            side = sideways(jnp.broadcast_to(peak, denom.shape)) * SCALE + jnp.log2(sideways(denom))
            high = side.astype(BF16).astype(F32)
            rest = side - high
            middle = rest.astype(BF16).astype(F32)
            lane = column_ids(level_rows(), HD)[None] % (HD // GROUPS)
            coded = jnp.where(lane == 0, high, jnp.where(lane == 1, middle, rest - middle))
            out[:, head, split:, :] = coded.astype(BF16)

    here = source[0] // C == chip

    @pl.when(jnp.logical_not(here))
    def _():
        run(False)

    @pl.when(here)
    def _():
        run(True)


def ask(host, source, meta, query, rows):
    return pl.pallas_call(
        ask_kernel,
        out_shape=jax.ShapeDtypeStruct((Z, X, piece_rows() + level_rows(), HD), BF16),
        in_specs=[smem()] * 3 + [vmem()] * 2,
        out_specs=vmem(),
        scratch_shapes=[pltpu.VMEM((C, BLOCK, 2 * HD), BF16)],
        compiler_params=params(),
        cost_estimate=pl.CostEstimate(
            flops=HALF * QUERY * C * BLOCK * HD * 6, bytes_accessed=1 << 20, transcendentals=HALF * QUERY * C * BLOCK
        ),
        name="ask",
    )(host, source, meta, query, rows)


def merge_kernel(received, out):
    split, step = piece_rows(), level_rows()
    pieces = received.shape[0]
    lane = lax.broadcasted_iota(jnp.int32, (HD, GROUPS * HD), 0)
    column = lax.broadcasted_iota(jnp.int32, (HD, GROUPS * HD), 1)
    width = HD // GROUPS
    adder = ((lane // width == column // HD) & (lane % width < 3)).astype(F32).astype(BF16)
    coded = received[:, split:, :].reshape(pieces * step, HD)
    levels = jnp.dot(coded, adder, preferred_element_type=F32).reshape(pieces, step, GROUPS * HD)
    for group in range(GROUPS):
        level = levels[:, :, group * HD : (group + 1) * HD]
        share = jnp.exp2(level - level.max(axis=0, keepdims=True))
        rows = slice(group * step, (group + 1) * step)
        numer = jnp.sum(share * received[:, rows, :].astype(F32), axis=0)
        merged = (numer / jnp.sum(share, axis=0)).astype(BF16)
        out[:, rows, :] = jnp.broadcast_to(merged[None], (pieces, step, HD))


def merge(received):
    return pl.pallas_call(
        merge_kernel,
        out_shape=jax.ShapeDtypeStruct((received.shape[0], piece_rows(), HD), BF16),
        in_specs=[vmem()],
        out_specs=vmem(),
        compiler_params=params(),
        name="merge",
    )(received)


def project_kernel(host, attended, weight, other, out):
    core = host[0] % C
    rows = [
        jnp.concatenate([attended[z, x] for x in range(X)], axis=1) for z in range(Z)
    ]
    rows = jnp.concatenate(rows, axis=0)
    first = pl.multiple_of(core * HALF * HD, HALF * HD)
    mine = jnp.dot(rows, weight[pl.ds(first, HALF * HD), :], preferred_element_type=F32)
    others = jnp.dot(rows, other[...], preferred_element_type=F32)
    out[pl.ds(core, 1)] = mine.astype(BF16)[None]
    out[pl.ds(1 - core, 1)] = others.astype(BF16)[None]


def project(host, attended, weight, other):
    return pl.pallas_call(
        project_kernel,
        out_shape=jax.ShapeDtypeStruct((C, QUERY, HD), BF16),
        in_specs=[smem()] + [vmem()] * 3,
        out_specs=vmem(),
        compiler_params=params(),
        name="project",
    )(host, attended, weight, other)


def total_kernel(shares, out):
    out[...] = jnp.sum(shares[...].astype(F32), axis=0).astype(BF16)


def total(shares):
    return pl.pallas_call(
        total_kernel,
        out_shape=jax.ShapeDtypeStruct(shares.shape[1:], BF16),
        in_specs=[vmem()],
        out_specs=vmem(),
        compiler_params=params(),
        name="total",
    )(shares)


def encode_kernel(host, meta, query, key, value, anchor, *rest):
    out, own_values, anchor_values = rest[-3:]
    own_values[...] = with_ones(value[...])
    anchor_values[...] = with_ones(anchor[BLOCK:, :])
    own_len = meta[host[0] % C]
    anchor_len = jnp.where(host[0] > 0, meta[C], 0)
    half = BLOCK // 2
    for head in range(out.shape[1] // HD):
        columns = slice(head * HD, (head + 1) * HD)
        for tile in range(2):
            rows = slice(tile * half, (tile + 1) * half)
            parts = [
                (key[rows, :], own_values[rows, :], causal(half)),
                (anchor[:BLOCK, :], anchor_values[...], column_ids(half, BLOCK) < anchor_len),
            ]
            if tile:
                parts.append((key[:half, :], own_values[:half, :], None))
            _, numer, denom = weigh(query[rows, columns], parts)
            live = lax.broadcasted_iota(jnp.int32, (half, HD), 0) + tile * half < own_len
            out[rows, columns] = jnp.where(live, numer / denom, 0.0).astype(BF16)


def encode(host, meta, query, key, value, anchor, part, parts, done=None):
    whole = pl.BlockSpec((BLOCK, HD), lambda i: (0, 0))
    heads = pl.BlockSpec((BLOCK, HEADS // parts * HD), lambda i: (0, part))
    given = () if done is None else (done,)
    return pl.pallas_call(
        encode_kernel,
        out_shape=jax.ShapeDtypeStruct(query.shape, BF16),
        grid=(1,),
        in_specs=[smem(), smem(), heads, whole, whole, pl.BlockSpec((2 * BLOCK, HD), lambda i: (0, 0))]
        + [anywhere()] * len(given),
        out_specs=heads,
        scratch_shapes=[pltpu.VMEM((BLOCK, 2 * HD), BF16)] * 2,
        input_output_aliases={6: 0} if given else {},
        compiler_params=params(),
        cost_estimate=pl.CostEstimate(
            flops=HEADS // parts * BLOCK * BLOCK * HD * 10,
            bytes_accessed=5 * BLOCK * HEADS // parts * HD,
            transcendentals=HEADS // parts * BLOCK * BLOCK * 2,
        ),
        name="encode",
    )(host, meta, query, key, value, anchor, *given)


def body(
    context_query,
    context_key,
    context_value,
    request_query,
    request_key,
    request_value,
    output_weight,
    block_lengths,
    query_host,
):
    pieces = Z * X
    core = lax.axis_index("c")
    host = lax.axis_index(("z", "x", "c")).astype(jnp.int32)[None]

    def neither(query, key, value):
        return blank()

    def request_only(query, key, value):
        return pack(host, query_host, query, lax.ppermute(query, "c", [(0, 1), (1, 0)]))

    def with_anchor(query, key, value):
        came = lax.ppermute(query, "c", [(0, 1), (1, 0)])
        return pack(host, query_host, query, came, key, lax.ppermute(value, "c", [(0, 1)]))

    chip = host[0] // C
    branch = jnp.where(chip == 0, 2, (chip == query_host[0] // C).astype(jnp.int32))
    branches = (neither, request_only, with_anchor)
    to_chips = lax.switch(branch, branches, request_query, context_key, context_value)
    to_chips = to_chips.reshape(pieces, -1, HD)
    from_chips = lax.all_to_all(to_chips, CHIPS, 0, 0, tiled=True)
    pair_rows = lax.all_gather(join(context_key, context_value, request_key, request_value), "c", axis=0)
    weight_half = lax.dynamic_slice_in_dim(output_weight, (1 - core) * HALF * HD, HALF * HD, 0)
    other_weight = lax.ppermute(weight_half, "c", [(0, 1), (1, 0)])
    meta = jnp.concatenate([lax.dynamic_slice_in_dim(block_lengths, host[0] // C * C, C, 0), block_lengths[:1]])
    from_chips, pair_rows, other_weight, meta = lax.optimization_barrier((from_chips, pair_rows, other_weight, meta))
    part = spread(query_host, from_chips)
    queries = lax.all_to_all(part, CHIPS, 0, 0, tiled=True)

    sums = ask(host, query_host, meta, queries.reshape(Z, X, -1, HD), pair_rows)
    met = lax.all_to_all(sums.reshape(pieces, -1, HD), CHIPS, 0, 0, tiled=True)
    anchor = lax.all_gather(queries[:, piece_rows() :, :].reshape(BLOCK, HD), "c", axis=0, tiled=True)
    context = (host, meta, context_query, context_key, context_value, anchor)
    encoded = encode(*context, 0, 2)
    met, encoded = lax.optimization_barrier((met, encoded))
    gathered = lax.all_to_all(merge(met), CHIPS, 0, 0, tiled=True)
    encoded_context = encode(*context, 1, 2, encoded)
    gathered, encoded_context = lax.optimization_barrier((gathered, encoded_context))
    shares = project(host, gathered.reshape(Z, X, -1, HD), output_weight, other_weight)
    blocks = lax.axis_size("head")
    shares = lax.all_to_all(shares.reshape(C * blocks, -1, HD), ("c", "head"), 0, 0, tiled=True)
    return (encoded_context, total(shares))


def solution(mesh):
    fine = Mesh(mesh.devices.reshape(Z, X, C, -1), ("z", "x", "c", "head"))
    ctx = ("z", "x", "c")
    placed = (P(ctx, "head"),) * 6 + (P("head", ctx), P(), P())
    return jax.shard_map(
        body,
        mesh=fine,
        in_specs=placed,
        out_specs=(P(ctx, "head"), P("head", ctx)),
        check_vma=False,
    )
```

```python
import functools

import jax
import jax.numpy as jnp
from jax import lax
from jax.experimental import pallas as pl
from jax.experimental.pallas import tpu as pltpu
from jax.sharding import Mesh, PartitionSpec as P

HD = 128
HEADS = 8
HALF = HEADS // 2
BLOCK = 512
QUERY = 256
Z, X, C = 8, 4, 2
SCALE = HD ** (-0.5) * 1.4426950408889634
NEG = -1e30
GROUPS = 4
BF16 = jnp.bfloat16
F32 = jnp.float32
CHIPS = ("z", "x")


def params(mib=32):
    return pltpu.CompilerParams(vmem_limit_bytes=mib * 1024 * 1024)


def smem():
    return pl.BlockSpec(memory_space=pltpu.SMEM)


def vmem():
    return pl.BlockSpec(memory_space=pltpu.VMEM)


def weigh(query, parts):
    scores = []
    for keys, _, seen in parts:
        score = lax.dot_general(query, keys, (((1,), (1,)), ((), ())), preferred_element_type=F32)
        scores.append(score if seen is None else jnp.where(seen, score, NEG))
    peak = scores[0].max(axis=1, keepdims=True)
    for score in scores[1:]:
        peak = jnp.maximum(peak, score.max(axis=1, keepdims=True))
    total = None
    for score, (_, values, _) in zip(scores, parts):
        weights = jnp.exp2((score - peak) * SCALE).astype(BF16)
        term = jnp.dot(weights, values, preferred_element_type=F32)
        total = term if total is None else total + term
    return peak, total[:, :HD], total[:, HD:]


def with_ones(values):
    return jnp.concatenate([values, jnp.ones(values.shape, BF16)], axis=1)


def column_ids(rows, cols):
    return lax.broadcasted_iota(jnp.int32, (rows, cols), 1)


def causal(size):
    return column_ids(size, size) <= lax.broadcasted_iota(jnp.int32, (size, size), 0)


def piece_rows():
    return QUERY // Z


def anchor_rows():
    return BLOCK // (Z * X)


def level_rows():
    return piece_rows() // GROUPS


def pack_kernel(with_request, with_anchor, host, source, *refs):
    refs = list(refs)
    core = host[0] % C
    query, came = (refs.pop(0), refs.pop(0)) if with_request else (None, None)
    key, value = (refs.pop(0), refs.pop(0)) if with_anchor else (None, None)
    out, query_half, packed, load_sems, store_sems = refs
    first = pl.multiple_of(core * HALF * HD, HALF * HD)
    split = piece_rows()

    def put(head, rows, column):
        packed[:, head, :split, :] = rows[:, pl.ds(column, HD)].reshape(Z, split, HD)
        store(head, (slice(None), head, slice(0, split))).start()

    def store(index, part):
        return pltpu.make_async_copy(packed.at[part], out.at[part], store_sems.at[index])

    if with_request:
        here = source[0] % C == core

        @pl.when(here)
        def _():
            loads = [
                pltpu.make_async_copy(
                    query.at[:, pl.ds(first + head * HD, HD)],
                    query_half.at[:, pl.ds(head * HD, HD)],
                    load_sems.at[head],
                )
                for head in range(HALF)
            ]
            for load in loads:
                load.start()
            for head, load in enumerate(loads):
                load.wait()
                put(head, query_half, head * HD)

        @pl.when(jnp.logical_not(here))
        def _():
            for head in range(HALF):
                put(head, came, first + head * HD)

    if with_anchor:
        for index, rows in enumerate((key, value)):

            @pl.when(core == index)
            def _():
                packed[:, :, split:, :] = rows[...].reshape(Z, X, anchor_rows(), HD)

        anchor_part = (slice(None), slice(None), slice(split, packed.shape[2]))
        store(HALF, anchor_part).start()
        store(HALF, anchor_part).wait()
    if with_request:
        for head in range(HALF):
            store(head, (slice(None), head, slice(0, split))).wait()


def pack(host, source, request, anchor):
    shape = (Z, X, piece_rows() + anchor_rows(), HD)
    return pl.pallas_call(
        functools.partial(pack_kernel, bool(request), bool(anchor)),
        out_shape=jax.ShapeDtypeStruct(shape, BF16),
        in_specs=[smem()] * 2 + [anywhere(), vmem()] * bool(request) + [vmem()] * len(anchor),
        out_specs=anywhere(),
        scratch_shapes=[
            pltpu.VMEM((QUERY, HALF * HD), BF16),
            pltpu.VMEM(shape, BF16),
            pltpu.SemaphoreType.DMA((HALF,)),
            pltpu.SemaphoreType.DMA((HALF + 1,)),
        ],
        compiler_params=params(),
        name="pack",
    )(host, source, *request, *anchor)


def blank_kernel(out):
    pass


def blank():
    shape = (Z, X, piece_rows() + anchor_rows(), HD)
    return pl.pallas_call(
        blank_kernel, out_shape=jax.ShapeDtypeStruct(shape, BF16), out_specs=anywhere(), name="blank"
    )()


def anywhere():
    return pl.BlockSpec(memory_space=pl.ANY)


def join_kernel(*refs):
    out, row = refs[-1], 0
    for ref in refs[:-1]:
        out[row : row + ref.shape[0], :] = ref[...]
        row += ref.shape[0]


def join(*arrays):
    rows = sum(a.shape[0] for a in arrays)
    return pl.pallas_call(
        join_kernel,
        out_shape=jax.ShapeDtypeStruct((rows, HD), BF16),
        grid=(1,),
        in_specs=[pl.BlockSpec(a.shape, lambda i: (0, 0)) for a in arrays],
        out_specs=pl.BlockSpec((rows, HD), lambda i: (0, 0)),
        compiler_params=params(),
        name="join",
    )(*arrays)


def spread_kernel(source, asked, anchor, out):
    split = piece_rows()
    out[:, :split, :] = jnp.broadcast_to(asked[:, :split, :], (out.shape[0], split, HD))
    out[:, split:, :] = jnp.broadcast_to(anchor[:, split:, :], (out.shape[0], out.shape[1] - split, HD))


def spread(source, received):
    pieces, rows, _ = received.shape
    return pl.pallas_call(
        spread_kernel,
        out_shape=jax.ShapeDtypeStruct(received.shape, BF16),
        grid_spec=pltpu.PrefetchScalarGridSpec(
            num_scalar_prefetch=1,
            grid=(1,),
            in_specs=[
                pl.BlockSpec((1, rows, HD), lambda i, source: (source[0] // C, 0, 0)),
                pl.BlockSpec((1, rows, HD), lambda i, source: (0, 0, 0)),
            ],
            out_specs=pl.BlockSpec(received.shape, lambda i, source: (0, 0, 0)),
        ),
        compiler_params=params(),
        name="spread",
    )(source, received, received)


def sideways(rows):
    rows = rows.reshape(Z, GROUPS, level_rows(), HD)
    group = column_ids(level_rows(), HD)[None] // (HD // GROUPS)
    side = rows[:, 0]
    for index in range(1, GROUPS):
        side = jnp.where(group == index, rows[:, index], side)
    return side


def ask_kernel(host, source, meta, query, rows, out, values):
    split = piece_rows()
    chip = host[0] // C
    for core in range(C):
        values[core] = with_ones(rows[core, BLOCK : 2 * BLOCK, :])

    def run(own):
        for head in range(HALF):
            asked = query[:, head, :split, :].reshape(QUERY, HD)
            parts = [
                (rows[core, :BLOCK, :], values[core], column_ids(QUERY, BLOCK) < meta[core])
                for core in range(C)
            ]
            if own:
                core = source[0] % C
                ask_key = rows[core, 2 * BLOCK : 2 * BLOCK + QUERY, :]
                ask_value = rows[core, 2 * BLOCK + QUERY :, :]
                parts.append((ask_key, with_ones(ask_value), causal(QUERY)))
            peak, numer, denom = weigh(asked, parts)
            out[:, head, :split, :] = (numer / denom).astype(BF16).reshape(Z, split, HD)
            side = sideways(jnp.broadcast_to(peak, denom.shape)) * SCALE + jnp.log2(sideways(denom))
            high = side.astype(BF16).astype(F32)
            rest = side - high
            middle = rest.astype(BF16).astype(F32)
            lane = column_ids(level_rows(), HD)[None] % (HD // GROUPS)
            coded = jnp.where(lane == 0, high, jnp.where(lane == 1, middle, rest - middle))
            out[:, head, split:, :] = coded.astype(BF16)

    here = source[0] // C == chip

    @pl.when(jnp.logical_not(here))
    def _():
        run(False)

    @pl.when(here)
    def _():
        run(True)


def ask(host, source, meta, query, rows):
    return pl.pallas_call(
        ask_kernel,
        out_shape=jax.ShapeDtypeStruct((Z, X, piece_rows() + level_rows(), HD), BF16),
        in_specs=[smem()] * 3 + [vmem()] * 2,
        out_specs=vmem(),
        scratch_shapes=[pltpu.VMEM((C, BLOCK, 2 * HD), BF16)],
        compiler_params=params(),
        cost_estimate=pl.CostEstimate(
            flops=HALF * QUERY * C * BLOCK * HD * 6, bytes_accessed=1 << 20, transcendentals=HALF * QUERY * C * BLOCK
        ),
        name="ask",
    )(host, source, meta, query, rows)


def merge_kernel(received, out):
    split, step = piece_rows(), level_rows()
    pieces = received.shape[0]
    lane = lax.broadcasted_iota(jnp.int32, (HD, GROUPS * HD), 0)
    column = lax.broadcasted_iota(jnp.int32, (HD, GROUPS * HD), 1)
    width = HD // GROUPS
    adder = ((lane // width == column // HD) & (lane % width < 3)).astype(F32).astype(BF16)
    coded = received[:, split:, :].reshape(pieces * step, HD)
    levels = jnp.dot(coded, adder, preferred_element_type=F32).reshape(pieces, step, GROUPS * HD)
    for group in range(GROUPS):
        level = levels[:, :, group * HD : (group + 1) * HD]
        share = jnp.exp2(level - level.max(axis=0, keepdims=True))
        rows = slice(group * step, (group + 1) * step)
        numer = jnp.sum(share * received[:, rows, :].astype(F32), axis=0)
        merged = (numer / jnp.sum(share, axis=0)).astype(BF16)
        out[:, rows, :] = jnp.broadcast_to(merged[None], (pieces, step, HD))


def merge(received):
    return pl.pallas_call(
        merge_kernel,
        out_shape=jax.ShapeDtypeStruct((received.shape[0], piece_rows(), HD), BF16),
        in_specs=[vmem()],
        out_specs=vmem(),
        compiler_params=params(),
        name="merge",
    )(received)


def project_kernel(host, attended, weight, other, out):
    core = host[0] % C
    rows = [
        jnp.concatenate([attended[z, x] for x in range(X)], axis=1) for z in range(Z)
    ]
    rows = jnp.concatenate(rows, axis=0)
    first = pl.multiple_of(core * HALF * HD, HALF * HD)
    mine = jnp.dot(rows, weight[pl.ds(first, HALF * HD), :], preferred_element_type=F32)
    others = jnp.dot(rows, other[...], preferred_element_type=F32)
    out[pl.ds(core, 1)] = mine.astype(BF16)[None]
    out[pl.ds(1 - core, 1)] = others.astype(BF16)[None]


def project(host, attended, weight, other):
    return pl.pallas_call(
        project_kernel,
        out_shape=jax.ShapeDtypeStruct((C, QUERY, HD), BF16),
        in_specs=[smem()] + [vmem()] * 3,
        out_specs=vmem(),
        compiler_params=params(),
        name="project",
    )(host, attended, weight, other)


def total_kernel(shares, out):
    out[...] = jnp.sum(shares[...].astype(F32), axis=0).astype(BF16)


def total(shares):
    return pl.pallas_call(
        total_kernel,
        out_shape=jax.ShapeDtypeStruct(shares.shape[1:], BF16),
        in_specs=[vmem()],
        out_specs=vmem(),
        compiler_params=params(),
        name="total",
    )(shares)


def encode_kernel(host, meta, query, key, value, anchor, *rest):
    out, own_values, anchor_values = rest[-3:]
    own_values[...] = with_ones(value[...])
    anchor_values[...] = with_ones(anchor[BLOCK:, :])
    own_len = meta[host[0] % C]
    anchor_len = jnp.where(host[0] > 0, meta[C], 0)
    half = BLOCK // 2
    for head in range(out.shape[1] // HD):
        columns = slice(head * HD, (head + 1) * HD)
        for tile in range(2):
            rows = slice(tile * half, (tile + 1) * half)
            parts = [
                (key[rows, :], own_values[rows, :], causal(half)),
                (anchor[:BLOCK, :], anchor_values[...], column_ids(half, BLOCK) < anchor_len),
            ]
            if tile:
                parts.append((key[:half, :], own_values[:half, :], None))
            _, numer, denom = weigh(query[rows, columns], parts)
            live = lax.broadcasted_iota(jnp.int32, (half, HD), 0) + tile * half < own_len
            out[rows, columns] = jnp.where(live, numer / denom, 0.0).astype(BF16)


def encode(host, meta, query, key, value, anchor, part, parts, done=None):
    whole = pl.BlockSpec((BLOCK, HD), lambda i: (0, 0))
    heads = pl.BlockSpec((BLOCK, HEADS // parts * HD), lambda i: (0, part))
    given = () if done is None else (done,)
    return pl.pallas_call(
        encode_kernel,
        out_shape=jax.ShapeDtypeStruct(query.shape, BF16),
        grid=(1,),
        in_specs=[smem(), smem(), heads, whole, whole, pl.BlockSpec((2 * BLOCK, HD), lambda i: (0, 0))]
        + [anywhere()] * len(given),
        out_specs=heads,
        scratch_shapes=[pltpu.VMEM((BLOCK, 2 * HD), BF16)] * 2,
        input_output_aliases={6: 0} if given else {},
        compiler_params=params(),
        cost_estimate=pl.CostEstimate(
            flops=HEADS // parts * BLOCK * BLOCK * HD * 10,
            bytes_accessed=5 * BLOCK * HEADS // parts * HD,
            transcendentals=HEADS // parts * BLOCK * BLOCK * 2,
        ),
        name="encode",
    )(host, meta, query, key, value, anchor, *given)


def body(
    context_query,
    context_key,
    context_value,
    request_query,
    request_key,
    request_value,
    output_weight,
    block_lengths,
    query_host,
):
    pieces = Z * X
    core = lax.axis_index("c")
    host = lax.axis_index(("z", "x", "c")).astype(jnp.int32)[None]

    def neither(query, key, value):
        return blank()

    def ours_and_theirs(query):
        return query, lax.ppermute(query, "c", [(0, 1), (1, 0)])

    def request_only(query, key, value):
        return pack(host, query_host, ours_and_theirs(query), ())

    def anchor_only(query, key, value):
        return pack(host, query_host, (), (key, lax.ppermute(value, "c", [(0, 1)])))

    def both(query, key, value):
        return pack(host, query_host, ours_and_theirs(query), (key, lax.ppermute(value, "c", [(0, 1)])))

    chip = host[0] // C
    branch = (chip == query_host[0] // C).astype(jnp.int32) + 2 * (chip == 0).astype(jnp.int32)
    branches = (neither, request_only, anchor_only, both)
    to_chips = lax.switch(branch, branches, request_query, context_key, context_value)
    to_chips = to_chips.reshape(pieces, -1, HD)
    from_chips = lax.all_to_all(to_chips, CHIPS, 0, 0, tiled=True)
    pair_rows = lax.all_gather(join(context_key, context_value, request_key, request_value), "c", axis=0)
    weight_half = lax.dynamic_slice_in_dim(output_weight, (1 - core) * HALF * HD, HALF * HD, 0)
    other_weight = lax.ppermute(weight_half, "c", [(0, 1), (1, 0)])
    meta = jnp.concatenate([lax.dynamic_slice_in_dim(block_lengths, host[0] // C * C, C, 0), block_lengths[:1]])
    from_chips, pair_rows, other_weight, meta = lax.optimization_barrier((from_chips, pair_rows, other_weight, meta))
    part = spread(query_host, from_chips)
    queries = lax.all_to_all(part, CHIPS, 0, 0, tiled=True)

    sums = ask(host, query_host, meta, queries.reshape(Z, X, -1, HD), pair_rows)
    met = lax.all_to_all(sums.reshape(pieces, -1, HD), CHIPS, 0, 0, tiled=True)
    anchor = lax.all_gather(queries[:, piece_rows() :, :].reshape(BLOCK, HD), "c", axis=0, tiled=True)
    context = (host, meta, context_query, context_key, context_value, anchor)
    encoded = encode(*context, 0, 2)
    met, encoded = lax.optimization_barrier((met, encoded))
    gathered = lax.all_to_all(merge(met), CHIPS, 0, 0, tiled=True)
    encoded_context = encode(*context, 1, 2, encoded)
    gathered, encoded_context = lax.optimization_barrier((gathered, encoded_context))
    shares = project(host, gathered.reshape(Z, X, -1, HD), output_weight, other_weight)
    blocks = lax.axis_size("head")
    shares = lax.all_to_all(shares.reshape(C * blocks, -1, HD), ("c", "head"), 0, 0, tiled=True)
    return (encoded_context, total(shares))


def solution(mesh):
    fine = Mesh(mesh.devices.reshape(Z, X, C, -1), ("z", "x", "c", "head"))
    ctx = ("z", "x", "c")
    placed = (P(ctx, "head"),) * 6 + (P("head", ctx), P(), P())
    return jax.shard_map(
        body,
        mesh=fine,
        in_specs=placed,
        out_specs=(P(ctx, "head"), P("head", ctx)),
        check_vma=False,
    )
```

```python
import functools

import jax
import jax.numpy as jnp
from jax import lax
from jax.experimental import pallas as pl
from jax.experimental.pallas import tpu as pltpu
from jax.sharding import Mesh, PartitionSpec as P

HD = 128
HEADS = 8
HALF = HEADS // 2
BLOCK = 512
QUERY = 256
Z, X, C = 8, 4, 2
SCALE = HD ** (-0.5) * 1.4426950408889634
NEG = -1e30
GROUPS = 4
BF16 = jnp.bfloat16
F32 = jnp.float32
CHIPS = ("z", "x")


def params(mib=32):
    return pltpu.CompilerParams(vmem_limit_bytes=mib * 1024 * 1024)


def smem():
    return pl.BlockSpec(memory_space=pltpu.SMEM)


def vmem():
    return pl.BlockSpec(memory_space=pltpu.VMEM)


def weigh(query, parts):
    scores = []
    for keys, _, seen in parts:
        score = lax.dot_general(query, keys, (((1,), (1,)), ((), ())), preferred_element_type=F32)
        scores.append(score if seen is None else jnp.where(seen, score, NEG))
    peak = scores[0].max(axis=1, keepdims=True)
    for score in scores[1:]:
        peak = jnp.maximum(peak, score.max(axis=1, keepdims=True))
    total = None
    for score, (_, values, _) in zip(scores, parts):
        weights = jnp.exp2((score - peak) * SCALE).astype(BF16)
        term = jnp.dot(weights, values, preferred_element_type=F32)
        total = term if total is None else total + term
    return peak, total[:, :HD], total[:, HD:]


def with_ones(values):
    return jnp.concatenate([values, jnp.ones(values.shape, BF16)], axis=1)


def column_ids(rows, cols):
    return lax.broadcasted_iota(jnp.int32, (rows, cols), 1)


def causal(size):
    return column_ids(size, size) <= lax.broadcasted_iota(jnp.int32, (size, size), 0)


def piece_rows():
    return QUERY // Z


def anchor_rows():
    return BLOCK // (Z * X)


def level_rows():
    return piece_rows() // GROUPS


def pack_own_kernel(source_core, query, out, query_half, packed, load_sems, store_sems):
    core = lax.axis_index("c")
    first = pl.multiple_of(core * HALF * HD, HALF * HD)

    @pl.when(core == source_core)
    def _():
        loads = [
            pltpu.make_async_copy(
                query.at[:, pl.ds(first + head * HD, HD)],
                query_half.at[:, pl.ds(head * HD, HD)],
                load_sems.at[head],
            )
            for head in range(HALF)
        ]
        stores = [
            pltpu.make_async_copy(packed.at[:, head], out.at[:, head, : piece_rows()], store_sems.at[head])
            for head in range(HALF)
        ]
        for load in loads:
            load.start()
        for head, (load, store) in enumerate(zip(loads, stores)):
            load.wait()
            packed[:, head] = query_half[:, head * HD : (head + 1) * HD].reshape(Z, piece_rows(), HD)
            store.start()
        for store in stores:
            store.wait()


def pack_own(source_core, query):
    return pl.pallas_call(
        functools.partial(pack_own_kernel, source_core),
        out_shape=jax.ShapeDtypeStruct((Z, X, piece_rows() + anchor_rows(), HD), BF16),
        in_specs=[anywhere()],
        out_specs=anywhere(),
        scratch_shapes=[
            pltpu.VMEM((QUERY, HALF * HD), BF16),
            pltpu.VMEM((Z, HALF, piece_rows(), HD), BF16),
            pltpu.SemaphoreType.DMA((HALF,)),
            pltpu.SemaphoreType.DMA((HALF,)),
        ],
        compiler_params=params(),
        name="pack_own",
    )(query)


def pack_came_kernel(source_core, came, given, out, packed, sems):
    core = lax.axis_index("c")
    first = pl.multiple_of(core * HALF * HD, HALF * HD)

    @pl.when(core != source_core)
    def _():
        stores = [
            pltpu.make_async_copy(packed.at[:, head], out.at[:, head, : piece_rows()], sems.at[head])
            for head in range(HALF)
        ]
        for head, store in enumerate(stores):
            packed[:, head] = came[:, pl.ds(first + head * HD, HD)].reshape(Z, piece_rows(), HD)
            store.start()
        for store in stores:
            store.wait()


def pack_came(source_core, came, packed):
    return pl.pallas_call(
        functools.partial(pack_came_kernel, source_core),
        out_shape=jax.ShapeDtypeStruct(packed.shape, BF16),
        in_specs=[vmem(), anywhere()],
        out_specs=anywhere(),
        input_output_aliases={1: 0},
        scratch_shapes=[pltpu.VMEM((Z, HALF, piece_rows(), HD), BF16), pltpu.SemaphoreType.DMA((HALF,))],
        compiler_params=params(),
        name="pack_came",
    )(came, packed)


def pack_anchor_kernel(key, value, given, out, packed, sem):
    for index, rows in enumerate((key, value)):

        @pl.when(lax.axis_index("c") == index)
        def _():
            packed[...] = rows[...].reshape(Z, X, anchor_rows(), HD)

    store = pltpu.make_async_copy(packed, out.at[:, :, piece_rows() :], sem)
    store.start()
    store.wait()


def pack_anchor(key, value, packed):
    return pl.pallas_call(
        pack_anchor_kernel,
        out_shape=jax.ShapeDtypeStruct(packed.shape, BF16),
        in_specs=[vmem()] * 2 + [anywhere()],
        out_specs=anywhere(),
        input_output_aliases={2: 0},
        scratch_shapes=[pltpu.VMEM((Z, X, anchor_rows(), HD), BF16), pltpu.SemaphoreType.DMA],
        compiler_params=params(),
        name="pack_anchor",
    )(key, value, packed)


def blank_kernel(out):
    pass


def blank():
    shape = (Z, X, piece_rows() + anchor_rows(), HD)
    return pl.pallas_call(
        blank_kernel, out_shape=jax.ShapeDtypeStruct(shape, BF16), out_specs=anywhere(), name="blank"
    )()


def anywhere():
    return pl.BlockSpec(memory_space=pl.ANY)


def join_kernel(*refs):
    out, row = refs[-1], 0
    for ref in refs[:-1]:
        out[row : row + ref.shape[0], :] = ref[...]
        row += ref.shape[0]


def join(*arrays):
    rows = sum(a.shape[0] for a in arrays)
    return pl.pallas_call(
        join_kernel,
        out_shape=jax.ShapeDtypeStruct((rows, HD), BF16),
        grid=(1,),
        in_specs=[pl.BlockSpec(a.shape, lambda i: (0, 0)) for a in arrays],
        out_specs=pl.BlockSpec((rows, HD), lambda i: (0, 0)),
        compiler_params=params(),
        name="join",
    )(*arrays)


def spread_kernel(source, asked, anchor, out):
    split = piece_rows()
    out[:, :split, :] = jnp.broadcast_to(asked[:, :split, :], (out.shape[0], split, HD))
    out[:, split:, :] = jnp.broadcast_to(anchor[:, split:, :], (out.shape[0], out.shape[1] - split, HD))


def spread(source, received):
    pieces, rows, _ = received.shape
    return pl.pallas_call(
        spread_kernel,
        out_shape=jax.ShapeDtypeStruct(received.shape, BF16),
        grid_spec=pltpu.PrefetchScalarGridSpec(
            num_scalar_prefetch=1,
            grid=(1,),
            in_specs=[
                pl.BlockSpec((1, rows, HD), lambda i, source: (source[0] // C, 0, 0)),
                pl.BlockSpec((1, rows, HD), lambda i, source: (0, 0, 0)),
            ],
            out_specs=pl.BlockSpec(received.shape, lambda i, source: (0, 0, 0)),
        ),
        compiler_params=params(),
        name="spread",
    )(source, received, received)


def sideways(rows):
    rows = rows.reshape(Z, GROUPS, level_rows(), HD)
    group = column_ids(level_rows(), HD)[None] // (HD // GROUPS)
    side = rows[:, 0]
    for index in range(1, GROUPS):
        side = jnp.where(group == index, rows[:, index], side)
    return side


def ask_kernel(meta, query, rows, out, values):
    split = piece_rows()
    for core in range(C):
        values[core] = with_ones(rows[core, BLOCK : 2 * BLOCK, :])

    def run(own):
        for head in range(HALF):
            asked = query[:, head, :split, :].reshape(QUERY, HD)
            parts = [
                (rows[core, :BLOCK, :], values[core], column_ids(QUERY, BLOCK) < meta[core])
                for core in range(C)
            ]
            if own:
                core = meta[C + 2]
                ask_key = rows[core, 2 * BLOCK : 2 * BLOCK + QUERY, :]
                ask_value = rows[core, 2 * BLOCK + QUERY :, :]
                parts.append((ask_key, with_ones(ask_value), causal(QUERY)))
            peak, numer, denom = weigh(asked, parts)
            out[:, head, :split, :] = (numer / denom).astype(BF16).reshape(Z, split, HD)
            side = sideways(jnp.broadcast_to(peak, denom.shape)) * SCALE + jnp.log2(sideways(denom))
            high = side.astype(BF16).astype(F32)
            rest = side - high
            middle = rest.astype(BF16).astype(F32)
            lane = column_ids(level_rows(), HD)[None] % (HD // GROUPS)
            coded = jnp.where(lane == 0, high, jnp.where(lane == 1, middle, rest - middle))
            out[:, head, split:, :] = coded.astype(BF16)

    here = meta[C + 1] != 0

    @pl.when(jnp.logical_not(here))
    def _():
        run(False)

    @pl.when(here)
    def _():
        run(True)


def ask(meta, query, rows):
    return pl.pallas_call(
        ask_kernel,
        out_shape=jax.ShapeDtypeStruct((Z, X, piece_rows() + level_rows(), HD), BF16),
        in_specs=[smem()] + [vmem()] * 2,
        out_specs=vmem(),
        scratch_shapes=[pltpu.VMEM((C, BLOCK, 2 * HD), BF16)],
        compiler_params=params(),
        cost_estimate=pl.CostEstimate(
            flops=HALF * QUERY * C * BLOCK * HD * 6, bytes_accessed=1 << 20, transcendentals=HALF * QUERY * C * BLOCK
        ),
        name="ask",
    )(meta, query, rows)


def merge_kernel(received, out):
    split, step = piece_rows(), level_rows()
    pieces = received.shape[0]
    lane = lax.broadcasted_iota(jnp.int32, (HD, GROUPS * HD), 0)
    column = lax.broadcasted_iota(jnp.int32, (HD, GROUPS * HD), 1)
    width = HD // GROUPS
    adder = ((lane // width == column // HD) & (lane % width < 3)).astype(F32).astype(BF16)
    coded = received[:, split:, :].reshape(pieces * step, HD)
    levels = jnp.dot(coded, adder, preferred_element_type=F32).reshape(pieces, step, GROUPS * HD)
    for group in range(GROUPS):
        level = levels[:, :, group * HD : (group + 1) * HD]
        share = jnp.exp2(level - level.max(axis=0, keepdims=True))
        rows = slice(group * step, (group + 1) * step)
        numer = jnp.sum(share * received[:, rows, :].astype(F32), axis=0)
        merged = (numer / jnp.sum(share, axis=0)).astype(BF16)
        out[:, rows, :] = jnp.broadcast_to(merged[None], (pieces, step, HD))


def merge(received):
    return pl.pallas_call(
        merge_kernel,
        out_shape=jax.ShapeDtypeStruct((received.shape[0], piece_rows(), HD), BF16),
        in_specs=[vmem()],
        out_specs=vmem(),
        compiler_params=params(),
        name="merge",
    )(received)


def project_kernel(attended, weight, other, out):
    core = lax.axis_index("c")
    rows = [
        jnp.concatenate([attended[z, x] for x in range(X)], axis=1) for z in range(Z)
    ]
    rows = jnp.concatenate(rows, axis=0)
    first = pl.multiple_of(core * HALF * HD, HALF * HD)
    mine = jnp.dot(rows, weight[pl.ds(first, HALF * HD), :], preferred_element_type=F32)
    others = jnp.dot(rows, other[...], preferred_element_type=F32)
    out[pl.ds(core, 1)] = mine.astype(BF16)[None]
    out[pl.ds(1 - core, 1)] = others.astype(BF16)[None]


def project(attended, weight, other):
    return pl.pallas_call(
        project_kernel,
        out_shape=jax.ShapeDtypeStruct((C, QUERY, HD), BF16),
        in_specs=[vmem()] * 3,
        out_specs=vmem(),
        compiler_params=params(),
        name="project",
    )(attended, weight, other)


def total_kernel(shares, out):
    out[...] = jnp.sum(shares[...].astype(F32), axis=0).astype(BF16)


def total(shares):
    return pl.pallas_call(
        total_kernel,
        out_shape=jax.ShapeDtypeStruct(shares.shape[1:], BF16),
        in_specs=[vmem()],
        out_specs=vmem(),
        compiler_params=params(),
        name="total",
    )(shares)


def encode_kernel(meta, query, key, value, anchor, *rest):
    out, own_values, anchor_values = rest[-3:]
    own_values[...] = with_ones(value[...])
    anchor_values[...] = with_ones(anchor[BLOCK:, :])
    own_len, anchor_len = meta[lax.axis_index("c")], meta[C]
    half = BLOCK // 2
    for head in range(out.shape[1] // HD):
        columns = slice(head * HD, (head + 1) * HD)
        for tile in range(2):
            rows = slice(tile * half, (tile + 1) * half)
            parts = [
                (key[rows, :], own_values[rows, :], causal(half)),
                (anchor[:BLOCK, :], anchor_values[...], column_ids(half, BLOCK) < anchor_len),
            ]
            if tile:
                parts.append((key[:half, :], own_values[:half, :], None))
            _, numer, denom = weigh(query[rows, columns], parts)
            live = lax.broadcasted_iota(jnp.int32, (half, HD), 0) + tile * half < own_len
            out[rows, columns] = jnp.where(live, numer / denom, 0.0).astype(BF16)


def encode(meta, query, key, value, anchor, part, parts, done=None):
    whole = pl.BlockSpec((BLOCK, HD), lambda i: (0, 0))
    heads = pl.BlockSpec((BLOCK, HEADS // parts * HD), lambda i: (0, part))
    given = () if done is None else (done,)
    return pl.pallas_call(
        encode_kernel,
        out_shape=jax.ShapeDtypeStruct(query.shape, BF16),
        grid=(1,),
        in_specs=[smem(), heads, whole, whole, pl.BlockSpec((2 * BLOCK, HD), lambda i: (0, 0))]
        + [anywhere()] * len(given),
        out_specs=heads,
        scratch_shapes=[pltpu.VMEM((BLOCK, 2 * HD), BF16)] * 2,
        input_output_aliases={5: 0} if given else {},
        compiler_params=params(),
        cost_estimate=pl.CostEstimate(
            flops=HEADS // parts * BLOCK * BLOCK * HD * 10,
            bytes_accessed=5 * BLOCK * HEADS // parts * HD,
            transcendentals=HEADS // parts * BLOCK * BLOCK * 2,
        ),
        name="encode",
    )(meta, query, key, value, anchor, *given)


def body(
    context_query,
    context_key,
    context_value,
    request_query,
    request_key,
    request_value,
    output_weight,
    block_lengths,
    query_host,
):
    pieces = Z * X
    core = lax.axis_index("c")
    host = lax.axis_index(("z", "x", "c")).astype(jnp.int32)[None]

    def neither(query, key, value):
        return blank()

    def request_only(source_core, query, key, value):
        came = lax.ppermute(query, "c", [(source_core, 1 - source_core)])
        return pack_came(source_core, came, pack_own(source_core, query))

    def with_anchor(packed, key, value):
        return pack_anchor(key, lax.ppermute(value, "c", [(0, 1)]), packed)

    def anchor_only(query, key, value):
        return with_anchor(blank(), key, value)

    def both(source_core, query, key, value):
        return with_anchor(request_only(source_core, query, key, value), key, value)

    chip = host[0] // C
    here = chip == query_host[0] // C
    branch = jnp.where(here, 1 + query_host[0] % C, 0) + (C + 1) * (chip == 0).astype(jnp.int32)
    branches = (
        (neither,)
        + tuple(functools.partial(request_only, source_core) for source_core in range(C))
        + (anchor_only,)
        + tuple(functools.partial(both, source_core) for source_core in range(C))
    )
    to_chips = lax.switch(branch, branches, request_query, context_key, context_value)
    to_chips = to_chips.reshape(pieces, -1, HD)
    from_chips = lax.all_to_all(to_chips, CHIPS, 0, 0, tiled=True)
    pair_rows = lax.all_gather(join(context_key, context_value, request_key, request_value), "c", axis=0)
    weight_half = lax.dynamic_slice_in_dim(output_weight, (1 - core) * HALF * HD, HALF * HD, 0)
    other_weight = lax.ppermute(weight_half, "c", [(0, 1), (1, 0)])
    anchor_len = jnp.where(host > 0, block_lengths[:1], 0)
    pair_lens = lax.dynamic_slice_in_dim(block_lengths, chip * C, C, 0)
    meta = jnp.concatenate([pair_lens, anchor_len, here[None].astype(jnp.int32), query_host % C])
    from_chips, pair_rows, other_weight, meta = lax.optimization_barrier((from_chips, pair_rows, other_weight, meta))
    part = spread(query_host, from_chips)
    queries = lax.all_to_all(part, CHIPS, 0, 0, tiled=True)

    sums = ask(meta, queries.reshape(Z, X, -1, HD), pair_rows)
    met = lax.all_to_all(sums.reshape(pieces, -1, HD), CHIPS, 0, 0, tiled=True)
    anchor = lax.all_gather(queries[:, piece_rows() :, :].reshape(BLOCK, HD), "c", axis=0, tiled=True)
    context = (meta, context_query, context_key, context_value, anchor)
    encoded = encode(*context, 0, 2)
    met, encoded = lax.optimization_barrier((met, encoded))
    gathered = lax.all_to_all(merge(met), CHIPS, 0, 0, tiled=True)
    encoded_context = encode(*context, 1, 2, encoded)
    gathered, encoded_context = lax.optimization_barrier((gathered, encoded_context))
    shares = project(gathered.reshape(Z, X, -1, HD), output_weight, other_weight)
    blocks = lax.axis_size("head")
    shares = lax.all_to_all(shares.reshape(C * blocks, -1, HD), ("c", "head"), 0, 0, tiled=True)
    return (encoded_context, total(shares))


def solution(mesh):
    fine = Mesh(mesh.devices.reshape(Z, X, C, -1), ("z", "x", "c", "head"))
    ctx = ("z", "x", "c")
    placed = (P(ctx, "head"),) * 6 + (P("head", ctx), P(), P())
    return jax.shard_map(
        body,
        mesh=fine,
        in_specs=placed,
        out_specs=(P(ctx, "head"), P("head", ctx)),
        check_vma=False,
    )
```
